128 devices in a mesh: ra: 8 (over z, x_lo), dec: 16 (over y, x_hi, core).
Axes of the slice: x: 4 (x_hi: 2, x_lo: 2; x = x_hi * 2 + x_lo), y: 4, z: 4, core: 2. Of those that a mesh axis runs over, the one named last changes fastest.
Arguments:
- forests: bfloat16 [16, 64, 128, 1024], P('ra', 'dec'), may hold values from -6 to 6
- resolution: float32 [16, 64, 128], P('ra', 'dec'), may hold values from 0.3 to 1.2
- pixel_range: int32 [16, 64, 2, 128], P('ra', 'dec'), may hold values from 0 to 1024, as said below
- block_pairs: int32 [8, 16, 40, 3], P('ra', 'dec'), may hold values from -1 to 7, as said below
- block_count: int32 [8, 16], P('ra', 'dec'), may hold values from 10 to 40, as said below
- separation_bin: int32 [8, 16, 40, 128, 128], P('ra', 'dec'), may hold values from 0 to 8
Outputs:
- tile_power: float32 [8, 16, 8, 128], P('ra', 'dec')
- sky_power: float32 [8, 128], replicated
The draws below stay inside these ranges and needn't reach their ends.
Inputs may be any that keep to these rules, and one draw needn't show every extreme that they name: `pixel_range`: lo < hi for every forest; at least 256 valid pixels. `block_pairs`: each device's list names every one of its own cells once with each of the five offsets (0, 0), (0, 1), (1, -1), (1, 0), (1, 1), in an order drawn from the seed. Slots at or past block_count are ignored. `block_count`: some device has all 40 slots live in every draw.
All inputs are finite; a program needn't handle non-finite values.
Results may differ from the reference program's by a relative error of at most 0.0037.
Values may be sent and summed in bfloat16 or wider, within the bound.
A program may use at most 64 MiB of HBM per device.

```python
import math
import jax
import jax.numpy as jnp
from jax import lax

CELLS_RA = 2
CELLS_DEC = 4
FPC = 128
NPIX = 1024
NSEP = 8
NKB = 128
BLOCKS = 40
ROWS = 16
COLS = 64
N_RA = 8
N_DEC = 16


def draw_pixel_range(key, part):
    first_key, second_key = jax.random.split(jax.random.fold_in(key, 11))
    shape = (CELLS_RA * N_RA, CELLS_DEC * N_DEC, 1, FPC)
    lower = jax.random.randint(first_key, shape, 0, NPIX // 4 + 1)
    extent = jax.random.randint(second_key, shape, NPIX // 2, NPIX + 1)
    upper = jnp.minimum(lower + extent, NPIX)
    return jnp.concatenate([lower, upper], axis=2).astype(jnp.int32)


def slot_helper(key):
    keys = jax.random.split(jax.random.fold_in(key, 23), 3)
    tiles = N_RA * N_DEC
    order_keys = jax.random.split(keys[0], tiles)
    orders = jax.vmap(lambda one_key: jax.random.permutation(one_key, BLOCKS))(order_keys)
    orders = orders.astype(jnp.int32).reshape(N_RA, N_DEC, BLOCKS)
    cells = orders // 5
    direction = orders % 5
    ra_step = (direction >= 2).astype(jnp.int32)
    dec_step = jnp.where(direction == 1, 1, jnp.where(direction >= 2, direction - 3, 0)).astype(jnp.int32)
    pairs = jnp.stack([cells, ra_step, dec_step], axis=-1).astype(jnp.int32)
    lowest = max(2, BLOCKS // 4)
    spread = jax.random.randint(keys[1], (N_RA, N_DEC), 0, 64)
    counts = lowest + (BLOCKS - lowest) * spread * spread // 4096
    fullest = jax.random.randint(keys[2], (), 0, tiles)
    flat_index = jnp.arange(tiles, dtype=jnp.int32).reshape(N_RA, N_DEC)
    counts = jnp.where(flat_index == fullest, BLOCKS, counts)
    return (pairs, counts.astype(jnp.int32))


def draw_block_pairs(key, part):
    return slot_helper(key)[0]


def draw_block_count(key, part):
    return slot_helper(key)[1]


def place_ends(array, rng, low, high):
    place = [jax.random.randint(jax.random.fold_in(rng, axis), (), 0, length) for axis, length in enumerate(array.shape)]
    longest = array.shape.index(max(array.shape))
    neighbour = place[:longest] + [(place[longest] + 1) % array.shape[longest]] + place[longest + 1:]
    return array.at[tuple(place)].set(low).at[tuple(neighbour)].set(high)


def levels(key, shape, pieces, least, largest):
    factor_of, own = 1.0, jax.random.fold_in(key, 6)
    for axis_at, parts in pieces:
        heights = jnp.exp(jax.random.uniform(jax.random.fold_in(own, axis_at), (parts,), jnp.float32, least / len(pieces), largest / len(pieces)))
        factor_of = factor_of * jnp.repeat(heights, shape[axis_at] // parts).reshape([-1 if axis == axis_at else 1 for axis in range(len(shape))])
    return factor_of


def scatter_about(rng, shape, deviation, bound, shards=(), held_as=jnp.bfloat16):
    level = levels(rng, shape, shards, -0.22, 0.18) if shards else 1.0
    array = jax.random.normal(rng, shape, jnp.float32) * deviation * level
    return jnp.minimum(jnp.maximum(array, -bound), bound).astype(held_as)


def setup_inputs(seed: int = 0) -> dict:
    seeds = jax.random.split(jax.random.key(seed), 7)
    return {
        "forests": scatter_about(seeds[0], (ROWS, COLS, FPC, NPIX), 1.0, 6.0, ((0, 8), (1, 16))),
        "resolution": jnp.clip(jnp.exp(math.log(1.2) - 1.3862944 * jax.random.uniform(seeds[1], (ROWS, COLS, FPC), jnp.float32) ** levels(seeds[1], (ROWS, COLS, FPC), ((0, 8), (1, 16)), -0.2, 0.2)), 0.3, 1.2),
        "pixel_range": draw_pixel_range(jax.random.fold_in(seeds[6], 71), 0),
        "block_pairs": draw_block_pairs(jax.random.fold_in(seeds[6], 71), 0),
        "block_count": draw_block_count(jax.random.fold_in(seeds[6], 71), 0),
        "separation_bin": place_ends(jax.random.randint(seeds[5], (N_RA, N_DEC, BLOCKS, FPC, FPC), 0, NSEP + 1), jax.random.fold_in(seeds[5], 1), 0, NSEP).astype(jnp.int32),
    }


def dft_table(length, n_modes):
    sample = jnp.arange(length, dtype=jnp.int32)[:, None]
    mode_index = jnp.arange(n_modes, dtype=jnp.int32)[None, :]
    angles = ((sample * mode_index) % length).astype(jnp.float32) * (2.0 * jnp.pi / length)
    return jnp.concatenate([jnp.cos(angles), jnp.sin(angles)], axis=1).astype(jnp.bfloat16)


def kbin_table(n_modes, n_bins):
    column = jnp.arange(2 * n_modes, dtype=jnp.int32) % n_modes
    which = column // (n_modes // n_bins)
    return (which[:, None] == jnp.arange(n_bins, dtype=jnp.int32)[None, :]).astype(jnp.float32)


def mask_pixels(flux, pixel_range):
    position = jnp.arange(flux.shape[-1], dtype=jnp.int32)
    lower = pixel_range[..., 0, :][..., None]
    upper = pixel_range[..., 1, :][..., None]
    inside = (position >= lower) & (position < upper)
    return jnp.where(inside, flux, jnp.zeros_like(flux))


def to_spectra(masked, widths, basis):
    length = basis.shape[0]
    n_modes = basis.shape[1] // 2
    raw = jnp.dot(masked, basis, preferred_element_type=jnp.float32)
    wavenum = jnp.arange(n_modes, dtype=jnp.float32) * (2.0 * jnp.pi / length)
    wavenum = jnp.concatenate([wavenum, wavenum])
    window = jnp.exp(-0.5 * (wavenum * widths[..., None]) ** 2)
    return (raw * window).astype(jnp.bfloat16)


def block_term(grid_flat, index_a, index_b, sep_bins):
    n_sep = NSEP
    per_cell = sep_bins.shape[0]
    left = lax.dynamic_index_in_dim(grid_flat, index_a.astype(jnp.int32), 0, keepdims=False)
    right = lax.dynamic_index_in_dim(grid_flat, index_b.astype(jnp.int32), 0, keepdims=False)
    onehot = (sep_bins[None, :, :] == jnp.arange(n_sep, dtype=jnp.int32)[:, None, None]).astype(jnp.bfloat16)
    mixed = jnp.dot(onehot.reshape(n_sep * per_cell, per_cell), right, preferred_element_type=jnp.float32)
    mixed = mixed.reshape(n_sep, per_cell, -1)
    block_sum = jnp.sum(mixed * left.astype(jnp.float32)[None], axis=1)
    pair_counts = jnp.sum(onehot.reshape(n_sep, -1).astype(jnp.float32), axis=1)
    return block_sum, pair_counts


def reference(forests, resolution, pixel_range, block_pairs, block_count, separation_bin):
    basis = dft_table(NPIX, NPIX // 2)

    def row_spectra(inputs):
        flux, widths, ranges = inputs
        return to_spectra(mask_pixels(flux, ranges), widths, basis)

    spectra = lax.map(row_spectra, (forests, resolution, pixel_range))
    padded = jnp.pad(spectra, ((1, 1), (1, 1), (0, 0), (0, 0)))
    cols_pad = COLS + 2
    grid_flat = padded.reshape(-1, FPC, NPIX)
    tiles = N_RA * N_DEC

    def one_tile(inputs):
        tile_index, entries, live_count, sep_bins = inputs
        tile_row = tile_index // N_DEC
        tile_col = tile_index % N_DEC

        def step(carry, slot_index):
            entry_row = entries[slot_index]
            row_a = tile_row * CELLS_RA + entry_row[0] // CELLS_DEC + 1
            col_a = tile_col * CELLS_DEC + entry_row[0] % CELLS_DEC + 1
            index_a = row_a * cols_pad + col_a
            index_b = (row_a + entry_row[1]) * cols_pad + col_a + entry_row[2]
            block_sum, counts = block_term(grid_flat, index_a, index_b, sep_bins[slot_index])
            is_live = (slot_index < live_count).astype(jnp.float32)
            return (carry[0] + is_live * block_sum, carry[1] + is_live * counts), None

        start_value = (jnp.zeros((NSEP, NPIX), jnp.float32), jnp.zeros((NSEP,), jnp.float32))
        (sums, counts), _ = lax.scan(step, start_value, jnp.arange(BLOCKS, dtype=jnp.int32))
        binned = jnp.dot(sums, kbin_table(NPIX // 2, NKB), precision=lax.Precision.HIGHEST)
        return binned, counts

    binned, counts = lax.map(one_tile, (jnp.arange(tiles, dtype=jnp.int32), block_pairs.reshape(tiles, BLOCKS, 3), block_count.reshape(tiles), separation_bin.reshape(tiles, BLOCKS, FPC, FPC)))
    tile_power = (binned / (FPC * NPIX)).reshape(N_RA, N_DEC, NSEP, NKB)
    summed = jnp.sum(binned, axis=0)
    all_counts = jnp.sum(counts, axis=0)
    sky_power = summed / jnp.maximum(all_counts, 1.0)[:, None]
    return tile_power, sky_power
```

```python
import functools

import jax
import jax.numpy as jnp
import ml_dtypes
import numpy as np
from jax import lax
from jax.experimental import pallas as pl
from jax.experimental.pallas import tpu as pltpu
from jax.sharding import PartitionSpec as P

MESH = pl.DeviceIdType.MESH
NSEP = 8
NKB = 128
FPC = 128
NPIX = 1024
MODES = NPIX // 2
STRIDE = 6
TILE = 256
F32 = jnp.float32
BF16 = jnp.bfloat16


def dft_table():
    sample = np.arange(NPIX, dtype=np.int64)[:, None]
    mode = np.arange(MODES, dtype=np.int64)[None, :]
    angles = (sample * mode % NPIX).astype(np.float64) * (2.0 * np.pi / NPIX)
    table = np.concatenate([np.cos(angles), np.sin(angles)], axis=1)
    return table.astype(np.float32).astype(ml_dtypes.bfloat16)


def at(row, col):
    return row * STRIDE + col + 1


def kernel(
    n_ra, n_dec,
    forests, resolution, pixel_range, pairs, count, sep_hbm, basis_hbm,
    tile_out, sky_out,
    flux, basis, sep, spec, masked, onehot, acc, cacc, inv_v, inv_s, pay, pay2, box1, box2,
    load_sem, halo_sem, send_sem, sent1, got1, sent2, got2,
):
    p = lax.axis_index("ra")
    q = lax.axis_index("dec")
    odd = lax.rem(q, 2) == 1
    even = jnp.logical_not(odd)
    above, below = p < n_ra - 1, p > 0
    right, left = q < n_dec - 1, q > 0

    loads = [pltpu.make_async_copy(basis_hbm, basis, load_sem.at[0])]
    for k in range(4):
        cells = pl.ds(2 * (k % 2), 2)
        loads.append(pltpu.make_async_copy(
            forests.at[k // 2, cells], flux.at[pl.ds(2 * k, 2)], load_sem.at[1 + k]))
    loads.append(pltpu.make_async_copy(sep_hbm.at[0, 0], sep, load_sem.at[5]))
    loads[1].start()
    loads[0].start()
    for load in loads[2:]:
        load.start()

    barrier = pltpu.get_barrier_semaphore()
    for k in range(1, n_dec):
        pl.semaphore_signal(barrier, inc=1, device_id=(p, lax.rem(q + k, n_dec)), device_id_type=MESH)
    for k in range(1, n_ra):
        pl.semaphore_signal(barrier, inc=1, device_id=(lax.rem(p + k, n_ra), q), device_id_type=MESH)
    expected = jnp.int32(n_dec + n_ra - 2)
    for ok, dp, dq in (
        (above & right, 1, 1), (above & left, 1, -1), (below & right, -1, 1), (below & left, -1, -1),
    ):
        @pl.when(ok)
        def _():
            pl.semaphore_signal(barrier, inc=1, device_id=(p + dp, q + dq), device_id_type=MESH)
        expected += ok.astype(jnp.int32)

    entry = pairs[0, 0]
    step = jnp.where(entry[:, 1:2] == 0, entry[:, 2:3], entry[:, 2:3] + 3)
    code = entry[:, 0:1] * 5 + step
    slots = code.shape[0]
    hit = code == lax.broadcasted_iota(jnp.int32, (slots, 128), 1)
    slot_id = lax.broadcasted_iota(jnp.int32, (slots, 128), 0)
    inverse = jnp.max(jnp.where(hit, slot_id, 0), axis=0, keepdims=True)
    inv_v[...] = jnp.broadcast_to(inverse, inv_v.shape)
    to_smem = pltpu.make_async_copy(inv_v, inv_s, load_sem.at[6])
    to_smem.start()
    live_count = count[0, 0]

    blank = jnp.zeros((FPC, NPIX), BF16)
    for gone, cells in (
        (jnp.logical_not(above), [at(2, c) for c in range(-1, 5)]),
        (jnp.logical_not(right), [at(0, 4), at(1, 4), at(2, 4)]),
        (jnp.logical_not(left), [at(1, -1), at(2, -1)]),
    ):
        @pl.when(gone)
        def _():
            for cell in cells:
                spec[cell] = blank
    acc[...] = jnp.zeros_like(acc)
    cacc[...] = jnp.zeros_like(cacc)

    def send(source, target, sem, dp, dq):
        return pltpu.make_async_remote_copy(
            src_ref=spec.at[source], dst_ref=spec.at[target],
            send_sem=send_sem.at[sem], recv_sem=halo_sem.at[target],
            device_id=(p + dp, q + dq), device_id_type=MESH)

    def arrived(target):
        send(target, target, 0, 0, 0).wait_recv()

    down = [(send(at(0, c), at(2, c), c, -1, 0), below) for c in range(4)]
    down_left = (send(at(0, 0), at(2, 4), 4, -1, -1), below & left & even)
    down_right = (send(at(0, 3), at(2, -1), 5, -1, 1), below & right & odd)
    side = [
        (send(at(0, 0), at(0, 4), 6, 0, -1), left),
        (send(at(1, 0), at(1, 4), 7, 0, -1), left),
        (send(at(1, 3), at(1, -1), 8, 0, 1), right),
    ]
    pass_left = (send(at(2, 0), at(2, 4), 9, 0, -1), above & odd)
    pass_right = (send(at(2, 3), at(2, -1), 10, 0, 1), above & even)

    def start(entry):
        copy, ok = entry

        @pl.when(ok)
        def _():
            copy.start()

    widths = jnp.transpose(jnp.concatenate([resolution[0], resolution[1]], axis=0))
    bounds = [pixel_range[r, c] for r in range(2) for c in range(4)]
    bounds = jnp.transpose(jnp.concatenate(bounds, axis=0))
    position = lax.broadcasted_iota(jnp.int32, (FPC, NPIX), 1)
    wave = lax.broadcasted_iota(jnp.int32, (1, MODES), 1).astype(F32) * (2.0 * np.pi / NPIX)

    def spectra(k):
        loads[1 + k].wait()
        windows = []
        for h in range(2):
            cell = 2 * k + h
            low, high = bounds[:, 2 * cell:2 * cell + 1], bounds[:, 2 * cell + 1:2 * cell + 2]
            inside = (position >= low) & (position < high)
            masked[pl.ds(h * FPC, FPC)] = jnp.where(inside, flux[cell].astype(F32), 0.0).astype(BF16)
            windows.append(jnp.exp(-0.5 * (wave * widths[:, cell:cell + 1]) ** 2))
        if k == 0:
            loads[0].wait()
        for n in range(NPIX // TILE):
            cols = pl.ds(n * TILE, TILE)
            raw = jnp.dot(masked[...], basis[:, cols], preferred_element_type=F32)
            first = n * TILE % MODES
            for h in range(2):
                cell = at(k // 2, 2 * (k % 2) + h)
                value = raw[h * FPC:(h + 1) * FPC] * windows[h][:, first:first + TILE]
                spec[cell, :, cols] = value.astype(BF16)

    spectra(0)
    pl.semaphore_wait(barrier, expected)
    for entry in (down[0], down[1], down_left, side[0]):
        start(entry)
    spectra(1)
    for entry in (down[3], down[2], down_right):
        start(entry)
    spectra(2)
    start(side[1])
    spectra(3)
    start(side[2])

    loads[5].wait()
    to_smem.wait()

    def pair_up(a, b, first_code, n):
        for k in range(n):
            slot = inv_s[0, first_code + k]
            dead = jnp.where(slot < live_count, 0, 16)
            which = (sep[slot] + dead).astype(F32).astype(BF16)
            for t in range(NSEP):
                ones = jnp.where(which == jnp.asarray(t, BF16), jnp.asarray(1, BF16), jnp.asarray(0, BF16))
                onehot[pl.ds(t * FPC, FPC), pl.ds(k * FPC, FPC)] = ones
                cacc[t] += jnp.sum(ones.astype(F32).reshape(16, 8, FPC), axis=0)
        for m in range(NPIX // TILE):
            cols = pl.ds(m * TILE, TILE)
            partner = spec[pl.ds(b, n), :, cols].reshape(n * FPC, TILE)
            own = spec[a, :, cols].astype(F32).reshape(1, 16, 8, TILE)
            mixed = jnp.dot(onehot[:, :n * FPC], partner, preferred_element_type=F32)
            acc[:, :, cols] += jnp.sum(mixed.reshape(NSEP, 16, 8, TILE) * own, axis=1)

    def code_of(row, col, offset):
        return (row * 4 + col) * 5 + offset

    @pl.loop(0, 6)
    def _(k):
        row, col = k // 3, k % 3
        pair_up(at(row, col), at(row, col), code_of(row, col, 0), 2)

    @pl.loop(1, 3)
    def _(col):
        pair_up(at(0, col), at(1, col - 1), code_of(0, col, 2), 3)

    @pl.loop(0, 2)
    def _(k):
        col = 3 * k
        pair_up(at(0, col), at(1, col - k), code_of(0, col, 3 - k), 2)

    @pl.loop(0, 2)
    def _(row):
        pair_up(at(row, 3), at(row, 3), code_of(row, 3, 0), 1)

    for entry, cell in ((pass_left, at(2, 0)), (pass_right, at(2, 3))):
        @pl.when(entry[1])
        def _():
            arrived(cell)
            entry[0].start()

    for ok, cell in ((right, at(0, 4)), (right, at(1, 4)), (left, at(1, -1))):
        @pl.when(ok)
        def _():
            arrived(cell)

    @pl.loop(0, 2)
    def _(row):
        pair_up(at(row, 3), at(row, 4), code_of(row, 3, 1), 1)

    @pl.loop(0, 2)
    def _(k):
        col = 3 * k
        pair_up(at(0, col), at(1, col - 1 + 2 * k), code_of(0, col, 2 + 2 * k), 1)

    for ok, cell in (
        (above & even, at(2, 0)), (above, at(2, 1)), (above, at(2, 2)), (above & odd, at(2, 3)),
        (above & left, at(2, -1)), (above & right, at(2, 4)),
    ):
        @pl.when(ok)
        def _():
            arrived(cell)

    @pl.loop(0, 4)
    def _(col):
        pair_up(at(1, col), at(2, col - 1), code_of(1, col, 2), 3)

    column = lax.broadcasted_iota(jnp.int32, (NPIX, NKB), 0) % MODES
    which = column // (MODES // NKB) == lax.broadcasted_iota(jnp.int32, (NPIX, NKB), 1)
    table = jnp.where(which, 1.0, 0.0).astype(BF16)
    rest = acc[...].reshape(NSEP * 8, NPIX)
    folded = jnp.zeros((NSEP * 8, NKB), F32)
    for _ in range(3):
        part = rest.astype(BF16)
        folded += jnp.dot(part, table, preferred_element_type=F32)
        rest = rest - part.astype(F32)
    binned = jnp.sum(folded.reshape(NSEP, 8, NKB), axis=1)
    tile_out[0, 0] = binned * (1.0 / (FPC * NPIX))
    pay[0] = binned
    pay[1] = jnp.sum(cacc[...], axis=1)

    def everyone(source, box, mine, size, sent, got, peer):
        box[mine] = source[...]

        def copy(k):
            return pltpu.make_async_remote_copy(
                src_ref=source, dst_ref=box.at[mine], send_sem=sent.at[k], recv_sem=got.at[mine],
                device_id=peer(lax.rem(mine + k, size)), device_id_type=MESH)

        for k in range(1, size):
            copy(k).start()
        for k in range(1, size):
            other = lax.rem(mine + k, size)
            pltpu.make_async_remote_copy(
                src_ref=source, dst_ref=box.at[other], send_sem=sent.at[k], recv_sem=got.at[other],
                device_id=peer(other), device_id_type=MESH).wait_recv()
        total = box[0]
        for k in range(1, size):
            total = total + box[k]
        return total, [copy(k) for k in range(1, size)]

    total, first = everyone(pay, box1, q, n_dec, sent1, got1, lambda k: (p, k))
    pay2[...] = total
    total, second = everyone(pay2, box2, p, n_ra, sent2, got2, lambda k: (k, q))
    counts = jnp.sum(total[1], axis=1, keepdims=True)
    sky_out[...] = total[0] / jnp.maximum(counts, 1.0)

    for copy in first + second:
        copy.wait_send()
    for copy, ok in down + side + [down_left, down_right, pass_left, pass_right]:
        @pl.when(ok)
        def _():
            copy.wait_send()


def per_device(n_ra, n_dec, forests, resolution, pixel_range, pairs, count, sep):
    vmem = pl.BlockSpec(memory_space=pltpu.VMEM)
    smem = pl.BlockSpec(memory_space=pltpu.SMEM)
    anywhere = pl.BlockSpec(memory_space=pl.ANY)
    dma = pltpu.SemaphoreType.DMA
    return pl.pallas_call(
        functools.partial(kernel, n_ra, n_dec),
        out_shape=(
            jax.ShapeDtypeStruct((1, 1, NSEP, NKB), F32),
            jax.ShapeDtypeStruct((NSEP, NKB), F32),
        ),
        in_specs=[anywhere, vmem, vmem, vmem, smem, anywhere, anywhere],
        out_specs=(vmem, vmem),
        scratch_shapes=[
            pltpu.VMEM((8, FPC, NPIX), BF16),
            pltpu.VMEM((NPIX, NPIX), BF16),
            pltpu.VMEM(sep.shape[2:], jnp.int32),
            pltpu.VMEM((3 * STRIDE, FPC, NPIX), BF16),
            pltpu.VMEM((2 * FPC, NPIX), BF16),
            pltpu.VMEM((NSEP * FPC, 3 * FPC), BF16),
            pltpu.VMEM((NSEP, 8, NPIX), F32),
            pltpu.VMEM((NSEP, 8, FPC), F32),
            pltpu.VMEM((8, 128), jnp.int32),
            pltpu.SMEM((8, 128), jnp.int32),
            pltpu.VMEM((2, NSEP, NKB), F32),
            pltpu.VMEM((2, NSEP, NKB), F32),
            pltpu.VMEM((n_dec, 2, NSEP, NKB), F32),
            pltpu.VMEM((n_ra, 2, NSEP, NKB), F32),
            dma((7,)),
            dma((3 * STRIDE,)),
            dma((11,)),
            dma((n_dec,)),
            dma((n_dec,)),
            dma((n_ra,)),
            dma((n_ra,)),
        ],
        compiler_params=pltpu.CompilerParams(
            collective_id=0, has_side_effects=True, vmem_limit_bytes=56 * 1024 * 1024
        ),
        cost_estimate=pl.CostEstimate(flops=13_000_000_000, bytes_accessed=7_000_000, transcendentals=500_000),
    )(forests, resolution, pixel_range, pairs, count, sep, jnp.asarray(dft_table()))


def solution(mesh):
    n_ra, n_dec = mesh.shape["ra"], mesh.shape["dec"]
    return jax.shard_map(
        functools.partial(per_device, n_ra, n_dec),
        mesh=mesh,
        in_specs=(
            P("ra", "dec", None, None),
            P("ra", "dec", None),
            P("ra", "dec", None, None),
            P("ra", "dec", None, None),
            P("ra", "dec"),
            P("ra", "dec", None, None, None),
        ),
        out_specs=(P("ra", "dec", None, None), P()),
        check_vma=False,
    )
```

```python
import functools

import jax
import jax.numpy as jnp
import ml_dtypes
import numpy as np
from jax import lax
from jax.experimental import pallas as pl
from jax.experimental.pallas import tpu as pltpu
from jax.sharding import PartitionSpec as P

MESH = pl.DeviceIdType.MESH
NSEP = 8
NKB = 128
FPC = 128
NPIX = 1024
MODES = NPIX // 2
STRIDE = 6
TILE = 256
F32 = jnp.float32
BF16 = jnp.bfloat16


def dft_table():
    sample = np.arange(NPIX, dtype=np.int64)[:, None]
    mode = np.arange(MODES, dtype=np.int64)[None, :]
    angles = (sample * mode % NPIX).astype(np.float64) * (2.0 * np.pi / NPIX)
    table = np.concatenate([np.cos(angles), np.sin(angles)], axis=1)
    return table.astype(np.float32).astype(ml_dtypes.bfloat16)


def at(row, col):
    return row * STRIDE + col + 1


def kernel(
    n_ra, n_dec,
    forests, resolution, pixel_range, pairs, count, sep_hbm, basis_hbm,
    out,
    flux, basis, sep, spec, masked, onehot, acc, acc2, cacc, inv_v, inv_s, ship, shipped, lent, lent_in,
    pay, pay2, box1, box2, widths_v, range_v, pairs_v,
    load_sem, halo_sem, send_sem, sent1, got1, sent2, got2,
):
    p = lax.axis_index("ra")
    q = lax.axis_index("dec")
    odd = lax.rem(q, 2) == 1
    even = jnp.logical_not(odd)
    above, below = p < n_ra - 1, p > 0
    right, left = q < n_dec - 1, q > 0

    def load(source, target, k):
        return pltpu.make_async_copy(source, target, load_sem.at[k])

    flux_loads = [load(forests.at[k // 4, k % 4], flux.at[k], k) for k in range(8)]
    basis_load = load(basis_hbm, basis, 8)
    sep_load = load(sep_hbm.at[0, 0], sep, 9)
    small = [load(resolution, widths_v, 10), load(pixel_range, range_v, 11), load(pairs, pairs_v, 12)]
    to_smem = load(inv_v, inv_s, 13)
    for each in small[:2] + [flux_loads[0], flux_loads[3], basis_load, small[2]]:
        each.start()
    for k in (1, 2, 4, 7, 5, 6):
        flux_loads[k].start()
    sep_load.start()

    barrier = pltpu.get_barrier_semaphore()
    expected = jnp.int32(n_dec + n_ra - 2)
    for ok, dp, dq in (
        (above & right, 1, 1), (above & left, 1, -1), (below & right, -1, 1), (below & left, -1, -1),
    ):
        @pl.when(ok)
        def _():
            pl.semaphore_signal(barrier, inc=1, device_id=(p + dp, q + dq), device_id_type=MESH)
        expected += ok.astype(jnp.int32)
    for k in range(1, n_ra):
        pl.semaphore_signal(barrier, inc=1, device_id=(lax.rem(p + k, n_ra), q), device_id_type=MESH)
    for k in range(1, n_dec):
        pl.semaphore_signal(barrier, inc=1, device_id=(p, lax.rem(q + k, n_dec)), device_id_type=MESH)

    def send(source, target, sem, dp, dq):
        return pltpu.make_async_remote_copy(
            src_ref=spec.at[source], dst_ref=spec.at[target],
            send_sem=send_sem.at[sem], recv_sem=halo_sem.at[target],
            device_id=(p + dp, q + dq), device_id_type=MESH)

    def arrived(target, ok):
        @pl.when(ok)
        def _():
            send(target, target, 0, 0, 0).wait_recv()

    bins_there = 3 * STRIDE
    sums_back = bins_there + 1
    down = [(send(at(0, c), at(2, c), c, -1, 0), below) for c in range(4)]
    down_left = (send(at(0, 0), at(2, 4), 4, -1, -1), below & left & even)
    side_low = (send(at(0, 0), at(0, 4), 5, 0, -1), odd | (left & jnp.logical_not(below)))
    side_high = (send(at(1, 0), at(1, 4), 6, 0, -1), left)
    side_right = (send(at(1, 3), at(1, -1), 7, 0, 1), even)
    pass_left = (send(at(2, 0), at(2, 4), 8, 0, -1), above & odd)
    pass_right = (send(at(2, 3), at(2, -1), 9, 0, 1), above & even)
    pass_up = (send(at(2, 0), at(0, 4), 10, 1, -1), above & left & even)
    lend_bins = (pltpu.make_async_remote_copy(
        src_ref=ship, dst_ref=shipped, send_sem=send_sem.at[11], recv_sem=halo_sem.at[bins_there],
        device_id=(p, q - 1), device_id_type=MESH), even & left)
    give_back = (pltpu.make_async_remote_copy(
        src_ref=lent, dst_ref=lent_in, send_sem=send_sem.at[12], recv_sem=halo_sem.at[sums_back],
        device_id=(p, q + 1), device_id_type=MESH), odd & right)

    def start(entry):
        copy, ok = entry

        @pl.when(ok)
        def _():
            copy.start()

    def follow(before, entry):
        @pl.when(below)
        def _():
            before[0].wait_send()
            entry[0].start()

    small[0].wait()
    small[1].wait()
    widths = jnp.transpose(jnp.concatenate([widths_v[0], widths_v[1]], axis=0))
    bounds = jnp.transpose(jnp.concatenate([range_v[r, c] for r in range(2) for c in range(4)], axis=0))
    position = lax.broadcasted_iota(jnp.int32, (FPC, NPIX), 1)
    wave = lax.broadcasted_iota(jnp.int32, (1, MODES), 1).astype(F32) * (2.0 * np.pi / NPIX)

    def spectra(cells):
        windows = []
        for h, cell in enumerate(cells):
            flux_loads[cell].wait()
            low, high = bounds[:, 2 * cell:2 * cell + 1], bounds[:, 2 * cell + 1:2 * cell + 2]
            inside = (position >= low) & (position < high)
            masked[pl.ds(h * FPC, FPC)] = jnp.where(inside, flux[cell].astype(F32), 0.0).astype(BF16)
            windows.append(jnp.exp(-0.5 * (wave * widths[:, cell:cell + 1]) ** 2))
        if cells[0] == 0:
            basis_load.wait()
        for n in range(NPIX // TILE):
            cols = pl.ds(n * TILE, TILE)
            raw = jnp.dot(masked[...], basis[:, cols], preferred_element_type=F32)
            first = n * TILE % MODES
            for h, cell in enumerate(cells):
                value = raw[h * FPC:(h + 1) * FPC] * windows[h][:, first:first + TILE]
                spec[at(cell // 4, cell % 4), :, cols] = value.astype(BF16)

    spectra((0, 3))
    pl.semaphore_wait(barrier, expected)
    for entry in (down[0], down_left, side_low):
        start(entry)
    spectra((1, 2))
    spectra((4, 7))
    start(side_high)
    start(side_right)

    small[2].wait()
    ra_step, dec_step = pairs_v[0, 1], pairs_v[0, 2]
    code = pairs_v[0, 0] * 5 + jnp.where(ra_step == 0, dec_step, dec_step + 3)
    slots = code.shape[1]
    hit = code == lax.broadcasted_iota(jnp.int32, (slots, slots), 0)
    slot_id = lax.broadcasted_iota(jnp.int32, (slots, slots), 1)
    inverse = jnp.max(jnp.where(hit, slot_id, 0), axis=1, keepdims=True)
    inv_v[...] = jnp.broadcast_to(inverse, inv_v.shape)
    to_smem.start()
    live_count = count[0, 0]

    blank = jnp.zeros((FPC, NPIX), BF16)
    for gone, cells in (
        (jnp.logical_not(above), [at(2, c) for c in range(5)]),
        (jnp.logical_not(above) | even, [at(2, -1)]),
        (even, [at(1, -1)]),
        (jnp.logical_not(right), [at(0, 4), at(1, 4)]),
        (jnp.logical_not(right) & above, [at(2, 4)]),
    ):
        @pl.when(gone)
        def _():
            for cell in cells:
                spec[cell] = blank
    acc[...] = jnp.zeros_like(acc)
    cacc[...] = jnp.zeros_like(cacc)

    spectra((5, 6))
    to_smem.wait()
    sep_load.wait()

    def code_of(row, col, offset):
        return (row * 4 + col) * 5 + offset

    def bins_of(code):
        slot = inv_s[code, 0]
        return (sep[slot] + jnp.where(slot < live_count, 0, 16)).astype(F32).astype(BF16)

    @pl.when(lend_bins[1])
    def _():
        ship[0] = bins_of(code_of(0, 0, 2))
        ship[1] = bins_of(code_of(1, 0, 2))
        lend_bins[0].start()

    def spread(which, k, counted):
        for t in range(NSEP):
            ones = jnp.where(which == jnp.asarray(t, BF16), jnp.asarray(1, BF16), jnp.asarray(0, BF16))
            onehot[pl.ds(t * FPC, FPC), pl.ds(k * FPC, FPC)] = ones
            if counted:
                cacc[t] += jnp.sum(ones.astype(F32).reshape(16, 8, FPC), axis=0)

    def multiply(a, b, n, acc):
        for m in range(NPIX // TILE):
            cols = pl.ds(m * TILE, TILE)
            partner = spec[pl.ds(b, n), :, cols].reshape(n * FPC, TILE)
            own = spec[a, :, cols].astype(F32).reshape(1, 16, 8, TILE)
            mixed = jnp.dot(onehot[:, :n * FPC], partner, preferred_element_type=F32)
            acc[:, :, cols] += jnp.sum(mixed.reshape(NSEP, 16, 8, TILE) * own, axis=1)

    def pair_up(a, b, first_code, n):
        for k in range(n):
            spread(bins_of(first_code + k), k, True)
        multiply(a, b, n, acc)

    column = lax.broadcasted_iota(jnp.int32, (NPIX, NKB), 0) % MODES
    in_bin = column // (MODES // NKB) == lax.broadcasted_iota(jnp.int32, (NPIX, NKB), 1)
    table = jnp.where(in_bin, 1.0, 0.0).astype(BF16)

    def fold(acc):
        rest = acc[...].reshape(NSEP * 8, NPIX)
        folded = jnp.zeros((NSEP * 8, NKB), F32)
        for _ in range(3):
            part = rest.astype(BF16)
            folded += jnp.dot(part, table, preferred_element_type=F32)
            rest = rest - part.astype(F32)
        return jnp.sum(folded.reshape(NSEP, 8, NKB), axis=1)

    @pl.loop(0, 6)
    def _(k):
        row, col = k // 3, k % 3
        pair_up(at(row, col), at(row, col), code_of(row, col, 0), 2)

    follow(down[0], down[3])
    arrived(at(2, 0), above)
    for entry in (pass_up, pass_left):
        start(entry)

    @pl.loop(1, 3)
    def _(col):
        pair_up(at(0, col), at(1, col - 1), code_of(0, col, 2), 3)

    @pl.loop(0, 2)
    def _(k):
        col = 3 * k
        pair_up(at(0, col), at(1, col - k), code_of(0, col, 3 - k), 2)

    follow(down[3], down[1])
    arrived(at(2, 3), above)
    start(pass_right)
    arrived(at(1, 4), right)
    arrived(at(0, 4), right)

    @pl.when(give_back[1])
    def _():
        lend_bins[0].wait_recv()
        acc2[...] = jnp.zeros_like(acc2)

        @pl.loop(0, 2)
        def _(k):
            spread(shipped[k], 0, False)
            multiply(at(k, 4), at(k + 1, 3), 1, acc2)

        lent[...] = fold(acc2)
        give_back[0].start()

    @pl.loop(0, 2)
    def _(row):
        pair_up(at(row, 3), at(row, 3), code_of(row, 3, 0), 2)

    arrived(at(1, -1), odd)

    @pl.loop(0, 2)
    def _(k):
        col = 3 * k
        pair_up(at(0, col), at(1, col - 1 + 2 * k), code_of(0, col, 2 + 2 * k), 1)

    arrived(at(2, -1), above & odd)
    arrived(at(2, 4), above & right)

    @pl.loop(0, 2)
    def _(k):
        pair_up(at(1, 3 * k), at(2, 4 * k - 1), code_of(1, 3 * k, 2 + k), 2)

    follow(down[1], down[2])
    arrived(at(2, 1), above)

    @pl.loop(0, 2)
    def _(k):
        pair_up(at(1, 2 * k), at(2, 2 * k + 1), code_of(1, 2 * k, 4), 1)

    pair_up(at(1, 1), at(2, 0), code_of(1, 1, 2), 2)
    arrived(at(2, 2), above)
    pair_up(at(1, 2), at(2, 1), code_of(1, 2, 2), 2)

    @pl.loop(0, 2)
    def _(k):
        pair_up(at(1, 2 * k + 1), at(2, 2), code_of(1, 2 * k + 1, 4 - 2 * k), 1)

    pay[0] = fold(acc)

    @pl.when(lend_bins[1])
    def _():
        give_back[0].wait_recv()
        pay[0] += lent_in[...]

    pay[1] = jnp.sum(cacc[...], axis=1)

    def everyone(source, box, mine, size, sent, got, peer):
        box[mine] = source[...]

        def copy(k):
            return pltpu.make_async_remote_copy(
                src_ref=source, dst_ref=box.at[mine], send_sem=sent.at[k], recv_sem=got.at[mine],
                device_id=peer(lax.rem(mine + k, size)), device_id_type=MESH)

        for k in range(1, size):
            copy(k).start()
        for k in range(1, size):
            other = lax.rem(mine + k, size)
            pltpu.make_async_remote_copy(
                src_ref=source, dst_ref=box.at[other], send_sem=sent.at[k], recv_sem=got.at[other],
                device_id=peer(other), device_id_type=MESH).wait_recv()
        total = box[0]
        for k in range(1, size):
            total = total + box[k]
        return total, [copy(k) for k in range(1, size)]

    total, first = everyone(pay, box1, q, n_dec, sent1, got1, lambda k: (p, k))
    pay2[...] = total
    total, second = everyone(pay2, box2, p, n_ra, sent2, got2, lambda k: (k, q))
    counts = jnp.sum(total[1], axis=1, keepdims=True)
    out[0] = pay[0]
    out[1] = total[0] / jnp.maximum(counts, 1.0)

    for copy in first + second:
        copy.wait_send()
    for copy, ok in [
        down[2], down_left, side_low, side_high, side_right, pass_left, pass_right, pass_up, lend_bins, give_back
    ]:
        @pl.when(ok)
        def _():
            copy.wait_send()


def per_device(n_ra, n_dec, forests, resolution, pixel_range, pairs, count, sep):
    vmem = pl.BlockSpec(memory_space=pltpu.VMEM)
    smem = pl.BlockSpec(memory_space=pltpu.SMEM)
    anywhere = pl.BlockSpec(memory_space=pl.ANY)
    dma = pltpu.SemaphoreType.DMA
    slots = pairs.shape[2]
    pairs = jnp.transpose(pairs, (0, 3, 1, 2))
    both = pl.pallas_call(
        functools.partial(kernel, n_ra, n_dec),
        out_shape=jax.ShapeDtypeStruct((2, NSEP, NKB), F32),
        in_specs=[anywhere, anywhere, anywhere, anywhere, smem, anywhere, anywhere],
        out_specs=vmem,
        scratch_shapes=[
            pltpu.VMEM((8, FPC, NPIX), BF16),
            pltpu.VMEM((NPIX, NPIX), BF16),
            pltpu.VMEM(sep.shape[2:], jnp.int32),
            pltpu.VMEM((3 * STRIDE, FPC, NPIX), BF16),
            pltpu.VMEM((2 * FPC, NPIX), BF16),
            pltpu.VMEM((NSEP * FPC, 3 * FPC), BF16),
            pltpu.VMEM((NSEP, 8, NPIX), F32),
            pltpu.VMEM((NSEP, 8, NPIX), F32),
            pltpu.VMEM((NSEP, 8, FPC), F32),
            pltpu.VMEM((slots, 128), jnp.int32),
            pltpu.SMEM((slots, 128), jnp.int32),
            pltpu.VMEM((2, FPC, FPC), BF16),
            pltpu.VMEM((2, FPC, FPC), BF16),
            pltpu.VMEM((NSEP, NKB), F32),
            pltpu.VMEM((NSEP, NKB), F32),
            pltpu.VMEM((2, NSEP, NKB), F32),
            pltpu.VMEM((2, NSEP, NKB), F32),
            pltpu.VMEM((n_dec, 2, NSEP, NKB), F32),
            pltpu.VMEM((n_ra, 2, NSEP, NKB), F32),
            pltpu.VMEM(resolution.shape, F32),
            pltpu.VMEM(pixel_range.shape, jnp.int32),
            pltpu.VMEM(pairs.shape, jnp.int32),
            dma((14,)),
            dma((3 * STRIDE + 2,)),
            dma((13,)),
            dma((n_dec,)),
            dma((n_dec,)),
            dma((n_ra,)),
            dma((n_ra,)),
        ],
        compiler_params=pltpu.CompilerParams(
            collective_id=0, has_side_effects=True, vmem_limit_bytes=56 * 1024 * 1024
        ),
        cost_estimate=pl.CostEstimate(flops=13_000_000_000, bytes_accessed=7_000_000, transcendentals=500_000),
    )(forests, resolution, pixel_range, pairs, count, sep, jnp.asarray(dft_table()))
    return (both[0] * (1.0 / (FPC * NPIX))).reshape(1, 1, NSEP, NKB), both[1]


def solution(mesh):
    n_ra, n_dec = mesh.shape["ra"], mesh.shape["dec"]
    return jax.shard_map(
        functools.partial(per_device, n_ra, n_dec),
        mesh=mesh,
        in_specs=(
            P("ra", "dec", None, None),
            P("ra", "dec", None),
            P("ra", "dec", None, None),
            P("ra", "dec", None, None),
            P("ra", "dec"),
            P("ra", "dec", None, None, None),
        ),
        out_specs=(P("ra", "dec", None, None), P()),
        check_vma=False,
    )
```

```python
import functools

import jax
import jax.numpy as jnp
import ml_dtypes
import numpy as np
from jax import lax
from jax.experimental import pallas as pl
from jax.experimental.pallas import tpu as pltpu
from jax.sharding import PartitionSpec as P

MESH = pl.DeviceIdType.MESH
NSEP = 8
NKB = 128
FPC = 128
NPIX = 1024
MODES = NPIX // 2
STRIDE = 6
TILE = 256
F32 = jnp.float32
BF16 = jnp.bfloat16


def dft_table():
    sample = np.arange(NPIX, dtype=np.int64)[:, None]
    mode = np.arange(MODES, dtype=np.int64)[None, :]
    angles = (sample * mode % NPIX).astype(np.float64) * (2.0 * np.pi / NPIX)
    table = np.concatenate([np.cos(angles), np.sin(angles)], axis=1)
    return table.astype(np.float32).astype(ml_dtypes.bfloat16)


def at(row, col):
    return row * STRIDE + col + 1


def kernel(
    n_ra, n_dec,
    forests, resolution, pixel_range, pairs, count, sep_hbm, basis_hbm,
    out,
    flux, basis, sep, spec, masked, onehot, onehot2, acc, acc2, cacc, inv_v, inv_s, ship, shipped, lent, lent_in,
    pay, pay2, box1, box2, widths_v, range_v, pairs_v,
    load_sem, halo_sem, send_sem, sent1, got1, sent2, got2,
):
    p = lax.axis_index("ra")
    q = lax.axis_index("dec")
    odd = lax.rem(q, 2) == 1
    even = jnp.logical_not(odd)
    above, below = p < n_ra - 1, p > 0
    right, left = q < n_dec - 1, q > 0

    def load(source, target, k):
        return pltpu.make_async_copy(source, target, load_sem.at[k])

    flux_loads = [load(forests.at[k // 4, k % 4], flux.at[k], k) for k in range(8)]
    basis_load = load(basis_hbm, basis, 8)
    sep_load = load(sep_hbm.at[0, 0], sep, 9)
    small = [load(resolution, widths_v, 10), load(pixel_range, range_v, 11), load(pairs, pairs_v, 12)]
    to_smem = load(inv_v, inv_s, 13)
    for each in small[:2] + [flux_loads[0], flux_loads[3], basis_load, small[2]]:
        each.start()
    for k in (1, 2, 4, 7, 5, 6):
        flux_loads[k].start()
    sep_load.start()

    barrier = pltpu.get_barrier_semaphore()
    expected = jnp.int32(n_dec + n_ra - 2)
    for ok, dp, dq in (
        (above & right, 1, 1), (above & left, 1, -1), (below & right, -1, 1), (below & left, -1, -1),
    ):
        @pl.when(ok)
        def _():
            pl.semaphore_signal(barrier, inc=1, device_id=(p + dp, q + dq), device_id_type=MESH)
        expected += ok.astype(jnp.int32)
    for k in range(1, n_ra):
        pl.semaphore_signal(barrier, inc=1, device_id=(lax.rem(p + k, n_ra), q), device_id_type=MESH)
    for k in range(1, n_dec):
        pl.semaphore_signal(barrier, inc=1, device_id=(p, lax.rem(q + k, n_dec)), device_id_type=MESH)

    bins_there = 3 * STRIDE
    sums_back = bins_there + 1

    def send(source, target, sem, dp, dq):
        return pltpu.make_async_remote_copy(
            src_ref=spec.at[source], dst_ref=spec.at[target],
            send_sem=send_sem.at[sem], recv_sem=halo_sem.at[target],
            device_id=(p + dp, q + dq), device_id_type=MESH)

    def arrived(target, ok):
        @pl.when(ok)
        def _():
            send(target, target, 0, 0, 0).wait_recv()

    down = {c: (send(at(0, c), at(2, c), c, -1, 0), below) for c in (0, 1, 3)}

    def half(h):
        cols = pl.ds(h * MODES, MODES)
        return pltpu.make_async_remote_copy(
            src_ref=spec.at[at(0, 2), :, cols], dst_ref=spec.at[at(2, 2), :, cols],
            send_sem=send_sem.at[15 + h], recv_sem=halo_sem.at[bins_there + 2 + h],
            device_id=(p - 1, q), device_id_type=MESH)

    last = [(half(h), below) for h in range(2)]
    p_even = lax.rem(p, 2) == 0
    down_left = (send(at(0, 0), at(2, 4), 4, -1, -1), left & even & jnp.logical_not(p_even))
    to_relay = (send(at(0, 0), at(0, -1), 13, -2, 0), left & even & p_even & (p >= 2))
    relay = (send(at(0, -1), at(2, 4), 14, 1, -1), left & even & p_even & (p + 2 < n_ra))
    side_low = (send(at(0, 0), at(0, 4), 5, 0, -1), odd | (left & jnp.logical_not(below)))
    side_high = (send(at(1, 0), at(1, 4), 6, 0, -1), left)
    side_right = (send(at(1, 3), at(1, -1), 7, 0, 1), even)
    pass_left = (send(at(2, 0), at(2, 4), 8, 0, -1), above & odd)
    pass_right = (send(at(2, 3), at(2, -1), 9, 0, 1), above & even)
    pass_up = (send(at(2, 0), at(0, 4), 10, 1, -1), above & left & even)
    lend_bins = (pltpu.make_async_remote_copy(
        src_ref=ship, dst_ref=shipped, send_sem=send_sem.at[11], recv_sem=halo_sem.at[bins_there],
        device_id=(p, q - 1), device_id_type=MESH), even & left)
    give_back = (pltpu.make_async_remote_copy(
        src_ref=lent, dst_ref=lent_in, send_sem=send_sem.at[12], recv_sem=halo_sem.at[sums_back],
        device_id=(p, q + 1), device_id_type=MESH), odd & right)

    def start(entry):
        copy, ok = entry

        @pl.when(ok)
        def _():
            copy.start()

    def follow(before, entry):
        @pl.when(below)
        def _():
            before[0].wait_send()
            entry[0].start()

    small[0].wait()
    small[1].wait()
    widths = jnp.transpose(jnp.concatenate([widths_v[0], widths_v[1]], axis=0))
    bounds = jnp.transpose(jnp.concatenate([range_v[r, c] for r in range(2) for c in range(4)], axis=0))
    position = lax.broadcasted_iota(jnp.int32, (FPC, NPIX), 1)
    wave = lax.broadcasted_iota(jnp.int32, (1, MODES), 1).astype(F32) * (2.0 * np.pi / NPIX)

    def spectra(cells):
        windows = []
        for h, cell in enumerate(cells):
            flux_loads[cell].wait()
            low, high = bounds[:, 2 * cell:2 * cell + 1], bounds[:, 2 * cell + 1:2 * cell + 2]
            inside = (position >= low) & (position < high)
            masked[pl.ds(h * FPC, FPC)] = jnp.where(inside, flux[cell].astype(F32), 0.0).astype(BF16)
            windows.append(jnp.exp(-0.5 * (wave * widths[:, cell:cell + 1]) ** 2))
        if cells[0] == 0:
            basis_load.wait()
        for n in range(NPIX // TILE):
            cols = pl.ds(n * TILE, TILE)
            raw = jnp.dot(masked[...], basis[:, cols], preferred_element_type=F32)
            first = n * TILE % MODES
            for h, cell in enumerate(cells):
                value = raw[h * FPC:(h + 1) * FPC] * windows[h][:, first:first + TILE]
                spec[at(cell // 4, cell % 4), :, cols] = value.astype(BF16)

    spectra((0, 3))
    pl.semaphore_wait(barrier, expected)
    for entry in (down[0], down_left, to_relay, side_low):
        start(entry)
    spectra((1, 2))
    spectra((4, 7))
    start(side_high)
    start(side_right)

    small[2].wait()
    ra_step, dec_step = pairs_v[0, 1], pairs_v[0, 2]
    code = pairs_v[0, 0] * 5 + jnp.where(ra_step == 0, dec_step, dec_step + 3)
    slots = code.shape[1]
    hit = code == lax.broadcasted_iota(jnp.int32, (slots, slots), 0)
    slot_id = lax.broadcasted_iota(jnp.int32, (slots, slots), 1)
    inverse = jnp.max(jnp.where(hit, slot_id, 0), axis=1, keepdims=True)
    inv_v[...] = jnp.broadcast_to(inverse, inv_v.shape)
    to_smem.start()
    live_count = count[0, 0]

    blank = jnp.zeros((FPC, NPIX), BF16)
    for gone, cells in (
        (jnp.logical_not(above), [at(2, c) for c in range(5)]),
        (jnp.logical_not(above) | even, [at(2, -1)]),
        (even, [at(1, -1)]),
        (jnp.logical_not(right), [at(0, 4), at(1, 4)]),
        (jnp.logical_not(right) & above, [at(2, 4)]),
    ):
        @pl.when(gone)
        def _():
            for cell in cells:
                spec[cell] = blank
    acc[...] = jnp.zeros_like(acc)
    cacc[...] = jnp.zeros_like(cacc)

    spectra((5, 6))
    to_smem.wait()
    sep_load.wait()

    def code_of(row, col, offset):
        return (row * 4 + col) * 5 + offset

    def bins_of(code):
        slot = inv_s[code, 0]
        return (sep[slot] + jnp.where(slot < live_count, 0, 16)).astype(F32).astype(BF16)

    @pl.when(lend_bins[1])
    def _():
        ship[0] = bins_of(code_of(0, 0, 2))
        ship[1] = bins_of(code_of(1, 0, 2))
        lend_bins[0].start()

    def spread(which, k, counted, onehot):
        for t in range(NSEP):
            ones = jnp.where(which == jnp.asarray(t, BF16), jnp.asarray(1, BF16), jnp.asarray(0, BF16))
            onehot[pl.ds(t * FPC, FPC), pl.ds(k * FPC, FPC)] = ones
            if counted:
                cacc[t] += jnp.sum(ones.astype(F32).reshape(16, 8, FPC), axis=0)

    def multiply(a, b, n, acc):
        for m in range(NPIX // TILE):
            cols = pl.ds(m * TILE, TILE)
            partner = spec[pl.ds(b, n), :, cols].reshape(n * FPC, TILE)
            own = spec[a, :, cols].astype(F32).reshape(1, 16, 8, TILE)
            mixed = jnp.dot(onehot[:, :n * FPC], partner, preferred_element_type=F32)
            acc[:, :, cols] += jnp.sum(mixed.reshape(NSEP, 16, 8, TILE) * own, axis=1)

    def pair_up(a, b, first_code, n):
        for k in range(n):
            spread(bins_of(first_code + k), k, True, onehot)
        multiply(a, b, n, acc)

    column = lax.broadcasted_iota(jnp.int32, (NPIX, NKB), 0) % MODES
    in_bin = column // (MODES // NKB) == lax.broadcasted_iota(jnp.int32, (NPIX, NKB), 1)
    table = jnp.where(in_bin, 1.0, 0.0).astype(BF16)

    def fold(acc):
        rest = acc[...].reshape(NSEP * 8, NPIX)
        folded = jnp.zeros((NSEP * 8, NKB), F32)
        for _ in range(3):
            part = rest.astype(BF16)
            folded += jnp.dot(part, table, preferred_element_type=F32)
            rest = rest - part.astype(F32)
        return jnp.sum(folded.reshape(NSEP, 8, NKB), axis=1)

    @pl.loop(0, 6)
    def _(k):
        row, col = k // 3, k % 3
        pair_up(at(row, col), at(row, col), code_of(row, col, 0), 2)

    follow(down[0], down[3])
    arrived(at(0, -1), relay[1])
    start(relay)
    arrived(at(2, 0), above)
    for entry in (pass_up, pass_left):
        start(entry)

    @pl.loop(1, 3)
    def _(col):
        pair_up(at(0, col), at(1, col - 1), code_of(0, col, 2), 3)

    @pl.loop(0, 2)
    def _(k):
        col = 3 * k
        pair_up(at(0, col), at(1, col - k), code_of(0, col, 3 - k), 2)

    follow(down[3], down[1])
    arrived(at(2, 3), above)
    start(pass_right)
    arrived(at(1, 4), right)
    arrived(at(0, 4), right)

    @pl.when(give_back[1])
    def _():
        lend_bins[0].wait_recv()
        acc2[...] = jnp.zeros_like(acc2)

        @pl.loop(0, 2)
        def _(k):
            spread(shipped[k], 0, False, onehot)
            multiply(at(k, 4), at(k + 1, 3), 1, acc2)

        lent[...] = fold(acc2)
        give_back[0].start()

    @pl.loop(0, 2)
    def _(row):
        pair_up(at(row, 3), at(row, 3), code_of(row, 3, 0), 2)

    arrived(at(1, -1), odd)

    @pl.loop(0, 2)
    def _(k):
        col = 3 * k
        pair_up(at(0, col), at(1, col - 1 + 2 * k), code_of(0, col, 2 + 2 * k), 1)

    arrived(at(2, -1), above & odd)
    arrived(at(2, 4), above & right)

    @pl.loop(0, 2)
    def _(k):
        pair_up(at(1, 3 * k), at(2, 4 * k - 1), code_of(1, 3 * k, 2 + k), 2)

    follow(down[1], last[0])
    arrived(at(2, 1), above)

    @pl.loop(0, 2)
    def _(k):
        pair_up(at(1, 2 * k), at(2, 2 * k + 1), code_of(1, 2 * k, 4), 1)

    pair_up(at(1, 1), at(2, 0), code_of(1, 1, 2), 2)
    follow(last[0], last[1])

    for k, (col, offset) in enumerate(((2, 2), (2, 3), (1, 4), (3, 2))):
        spread(bins_of(code_of(1, col, offset)), k, True, onehot2)
    for h in range(2):
        @pl.when(above)
        def _():
            last[h][0].wait_recv()

        @pl.loop(0, MODES // TILE)
        def _(m):
            cols = pl.ds(pl.multiple_of(h * MODES + m * TILE, TILE), TILE)
            total = acc[:, :, cols]
            for col, b, n, lane in ((2, 1, 2, 0), (1, 2, 1, 2), (3, 2, 1, 3)):
                partner = spec[pl.ds(at(2, b), n), :, cols].reshape(n * FPC, TILE)
                own = spec[at(1, col), :, cols].astype(F32).reshape(1, 16, 8, TILE)
                ones = onehot2[:, lane * FPC:(lane + n) * FPC]
                mixed = jnp.dot(ones, partner, preferred_element_type=F32)
                total += jnp.sum(mixed.reshape(NSEP, 16, 8, TILE) * own, axis=1)
            acc[:, :, cols] = total

    pay[0] = fold(acc)

    @pl.when(lend_bins[1])
    def _():
        give_back[0].wait_recv()
        pay[0] += lent_in[...]

    pay[1] = jnp.sum(cacc[...], axis=1)

    def everyone(source, box, mine, size, sent, got, peer):
        box[mine] = source[...]

        def copy(k):
            return pltpu.make_async_remote_copy(
                src_ref=source, dst_ref=box.at[mine], send_sem=sent.at[k], recv_sem=got.at[mine],
                device_id=peer(lax.rem(mine + k, size)), device_id_type=MESH)

        for k in sorted(range(1, size), key=lambda k: abs(2 * k - size)):
            copy(k).start()
        for k in range(1, size):
            other = lax.rem(mine + k, size)
            pltpu.make_async_remote_copy(
                src_ref=source, dst_ref=box.at[other], send_sem=sent.at[k], recv_sem=got.at[other],
                device_id=peer(other), device_id_type=MESH).wait_recv()
        total = box[0]
        for k in range(1, size):
            total = total + box[k]
        return total, [copy(k) for k in range(1, size)]

    total, first = everyone(pay, box1, q, n_dec, sent1, got1, lambda k: (p, k))
    pay2[...] = total
    total, second = everyone(pay2, box2, p, n_ra, sent2, got2, lambda k: (k, q))
    counts = jnp.sum(total[1], axis=1, keepdims=True)
    out[0] = pay[0]
    out[1] = total[0] / jnp.maximum(counts, 1.0)

    for copy in first + second:
        copy.wait_send()
    for copy, ok in [
        last[1], to_relay, relay, down_left, side_low, side_high, side_right, pass_left, pass_right, pass_up, lend_bins, give_back
    ]:
        @pl.when(ok)
        def _():
            copy.wait_send()


def per_device(n_ra, n_dec, forests, resolution, pixel_range, pairs, count, sep):
    vmem = pl.BlockSpec(memory_space=pltpu.VMEM)
    smem = pl.BlockSpec(memory_space=pltpu.SMEM)
    anywhere = pl.BlockSpec(memory_space=pl.ANY)
    dma = pltpu.SemaphoreType.DMA
    slots = pairs.shape[2]
    pairs = jnp.transpose(pairs, (0, 3, 1, 2))
    both = pl.pallas_call(
        functools.partial(kernel, n_ra, n_dec),
        out_shape=jax.ShapeDtypeStruct((2, NSEP, NKB), F32),
        in_specs=[anywhere, anywhere, anywhere, anywhere, smem, anywhere, anywhere],
        out_specs=vmem,
        scratch_shapes=[
            pltpu.VMEM((8, FPC, NPIX), BF16),
            pltpu.VMEM((NPIX, NPIX), BF16),
            pltpu.VMEM(sep.shape[2:], jnp.int32),
            pltpu.VMEM((3 * STRIDE, FPC, NPIX), BF16),
            pltpu.VMEM((2 * FPC, NPIX), BF16),
            pltpu.VMEM((NSEP * FPC, 3 * FPC), BF16),
            pltpu.VMEM((NSEP * FPC, 4 * FPC), BF16),
            pltpu.VMEM((NSEP, 8, NPIX), F32),
            pltpu.VMEM((NSEP, 8, NPIX), F32),
            pltpu.VMEM((NSEP, 8, FPC), F32),
            pltpu.VMEM((slots, 128), jnp.int32),
            pltpu.SMEM((slots, 128), jnp.int32),
            pltpu.VMEM((2, FPC, FPC), BF16),
            pltpu.VMEM((2, FPC, FPC), BF16),
            pltpu.VMEM((NSEP, NKB), F32),
            pltpu.VMEM((NSEP, NKB), F32),
            pltpu.VMEM((2, NSEP, NKB), F32),
            pltpu.VMEM((2, NSEP, NKB), F32),
            pltpu.VMEM((n_dec, 2, NSEP, NKB), F32),
            pltpu.VMEM((n_ra, 2, NSEP, NKB), F32),
            pltpu.VMEM(resolution.shape, F32),
            pltpu.VMEM(pixel_range.shape, jnp.int32),
            pltpu.VMEM(pairs.shape, jnp.int32),
            dma((14,)),
            dma((3 * STRIDE + 4,)),
            dma((17,)),
            dma((n_dec,)),
            dma((n_dec,)),
            dma((n_ra,)),
            dma((n_ra,)),
        ],
        compiler_params=pltpu.CompilerParams(
            collective_id=0, has_side_effects=True, vmem_limit_bytes=56 * 1024 * 1024
        ),
        cost_estimate=pl.CostEstimate(flops=13_000_000_000, bytes_accessed=7_000_000, transcendentals=500_000),
    )(forests, resolution, pixel_range, pairs, count, sep, jnp.asarray(dft_table()))
    return (both[0] * (1.0 / (FPC * NPIX))).reshape(1, 1, NSEP, NKB), both[1]


def solution(mesh):
    n_ra, n_dec = mesh.shape["ra"], mesh.shape["dec"]
    return jax.shard_map(
        functools.partial(per_device, n_ra, n_dec),
        mesh=mesh,
        in_specs=(
            P("ra", "dec", None, None),
            P("ra", "dec", None),
            P("ra", "dec", None, None),
            P("ra", "dec", None, None),
            P("ra", "dec"),
            P("ra", "dec", None, None, None),
        ),
        out_specs=(P("ra", "dec", None, None), P()),
        check_vma=False,
    )
```

```python
import functools

import jax
import jax.numpy as jnp
import ml_dtypes
import numpy as np
from jax import lax
from jax.experimental import pallas as pl
from jax.experimental.pallas import tpu as pltpu
from jax.sharding import PartitionSpec as P

MESH = pl.DeviceIdType.MESH
NSEP = 8
NKB = 128
FPC = 128
NPIX = 1024
MODES = NPIX // 2
STRIDE = 6
TILE = 256
F32 = jnp.float32
BF16 = jnp.bfloat16


def dft_table():
    sample = np.arange(NPIX, dtype=np.int64)[:, None]
    mode = np.arange(MODES, dtype=np.int64)[None, :]
    angles = (sample * mode % NPIX).astype(np.float64) * (2.0 * np.pi / NPIX)
    table = np.concatenate([np.cos(angles), np.sin(angles)], axis=1)
    return table.astype(np.float32).astype(ml_dtypes.bfloat16)


def at(row, col):
    return row * STRIDE + col + 1


def kernel(
    n_ra, n_dec,
    forests, resolution, pixel_range, pairs, count, sep_hbm, basis_hbm,
    out,
    flux, basis, sep, spec, masked, onehot, onehot2, acc, acc2, cacc, inv_v, inv_s, ship, shipped, lent, lent_in,
    pay, pay2, box1, box2, widths_v, range_v, pairs_v,
    load_sem, halo_sem, send_sem, sent1, got1, sent2, got2,
):
    p = lax.axis_index("ra")
    q = lax.axis_index("dec")
    odd = lax.rem(q, 2) == 1
    even = jnp.logical_not(odd)
    above, below = p < n_ra - 1, p > 0
    right, left = q < n_dec - 1, q > 0

    def load(source, target, k):
        return pltpu.make_async_copy(source, target, load_sem.at[k])

    flux_loads = [load(forests.at[k // 4, k % 4], flux.at[k], k) for k in range(8)]
    basis_load = load(basis_hbm, basis, 8)
    sep_load = load(sep_hbm.at[0, 0], sep, 9)
    small = [load(resolution, widths_v, 10), load(pixel_range, range_v, 11), load(pairs, pairs_v, 12)]
    to_smem = load(inv_v, inv_s, 13)
    for each in small[:2] + [flux_loads[0], flux_loads[3], basis_load, small[2]]:
        each.start()
    for k in (1, 2, 4, 7, 5, 6):
        flux_loads[k].start()
    sep_load.start()

    barrier = pltpu.get_barrier_semaphore()
    expected = jnp.int32(n_dec + n_ra - 2)
    for ok, dp, dq in (
        (above & right, 1, 1), (above & left, 1, -1), (below & right, -1, 1), (below & left, -1, -1),
    ):
        @pl.when(ok)
        def _():
            pl.semaphore_signal(barrier, inc=1, device_id=(p + dp, q + dq), device_id_type=MESH)
        expected += ok.astype(jnp.int32)
    for k in range(1, n_ra):
        pl.semaphore_signal(barrier, inc=1, device_id=(lax.rem(p + k, n_ra), q), device_id_type=MESH)
    for k in range(1, n_dec):
        pl.semaphore_signal(barrier, inc=1, device_id=(p, lax.rem(q + k, n_dec)), device_id_type=MESH)

    bins_there = 3 * STRIDE
    sums_back = bins_there + 1

    def send(source, target, sem, dp, dq):
        return pltpu.make_async_remote_copy(
            src_ref=spec.at[source], dst_ref=spec.at[target],
            send_sem=send_sem.at[sem], recv_sem=halo_sem.at[target],
            device_id=(p + dp, q + dq), device_id_type=MESH)

    def arrived(target, ok):
        @pl.when(ok)
        def _():
            send(target, target, 0, 0, 0).wait_recv()

    down = {c: (send(at(0, c), at(2, c), c, -1, 0), below) for c in (0, 1, 3)}

    def half(h):
        cols = pl.ds(h * MODES, MODES)
        return pltpu.make_async_remote_copy(
            src_ref=spec.at[at(0, 2), :, cols], dst_ref=spec.at[at(2, 2), :, cols],
            send_sem=send_sem.at[15 + h], recv_sem=halo_sem.at[bins_there + 2 + h],
            device_id=(p - 1, q), device_id_type=MESH)

    last = [(half(h), below) for h in range(2)]
    p_even = lax.rem(p, 2) == 0
    down_left = (send(at(0, 0), at(2, 4), 4, -1, -1), left & even & jnp.logical_not(p_even))
    to_relay = (send(at(0, 0), at(0, -1), 13, -2, 0), left & even & p_even & (p >= 2))
    relay = (send(at(0, -1), at(2, 4), 14, 1, -1), left & even & p_even & (p + 2 < n_ra))
    side_low = (send(at(0, 0), at(0, 4), 5, 0, -1), odd | (left & jnp.logical_not(below)))
    side_high = (send(at(1, 0), at(1, 4), 6, 0, -1), left)
    side_right = (send(at(1, 3), at(1, -1), 7, 0, 1), even)
    pass_left = (send(at(2, 0), at(2, 4), 8, 0, -1), above & odd)
    pass_right = (send(at(2, 3), at(2, -1), 9, 0, 1), above & even)
    pass_up = (send(at(2, 0), at(0, 4), 10, 1, -1), above & left & even)
    lend_bins = (pltpu.make_async_remote_copy(
        src_ref=ship, dst_ref=shipped, send_sem=send_sem.at[11], recv_sem=halo_sem.at[bins_there],
        device_id=(p, q - 1), device_id_type=MESH), even & left)
    give_back = (pltpu.make_async_remote_copy(
        src_ref=lent, dst_ref=lent_in, send_sem=send_sem.at[12], recv_sem=halo_sem.at[sums_back],
        device_id=(p, q + 1), device_id_type=MESH), odd & right)

    def start(entry):
        copy, ok = entry

        @pl.when(ok)
        def _():
            copy.start()

    def follow(before, entry):
        @pl.when(below)
        def _():
            before[0].wait_send()
            entry[0].start()

    small[0].wait()
    small[1].wait()
    widths = jnp.transpose(jnp.concatenate([widths_v[0], widths_v[1]], axis=0))
    bounds = jnp.transpose(jnp.concatenate([range_v[r, c] for r in range(2) for c in range(4)], axis=0))
    position = lax.broadcasted_iota(jnp.int32, (FPC, NPIX), 1)
    wave = lax.broadcasted_iota(jnp.int32, (1, MODES), 1).astype(F32) * (2.0 * np.pi / NPIX)

    def spectra(cells):
        windows = []
        for h, cell in enumerate(cells):
            flux_loads[cell].wait()
            low, high = bounds[:, 2 * cell:2 * cell + 1], bounds[:, 2 * cell + 1:2 * cell + 2]
            inside = (position >= low) & (position < high)
            masked[pl.ds(h * FPC, FPC)] = jnp.where(inside, flux[cell].astype(F32), 0.0).astype(BF16)
            windows.append(jnp.exp(-0.5 * (wave * widths[:, cell:cell + 1]) ** 2))
        if cells[0] == 0:
            basis_load.wait()
        for n in range(NPIX // TILE):
            cols = pl.ds(n * TILE, TILE)
            raw = jnp.dot(masked[:len(cells) * FPC], basis[:, cols], preferred_element_type=F32)
            first = n * TILE % MODES
            for h, cell in enumerate(cells):
                value = raw[h * FPC:(h + 1) * FPC] * windows[h][:, first:first + TILE]
                spec[at(cell // 4, cell % 4), :, cols] = value.astype(BF16)

    spectra((0,))
    pl.semaphore_wait(barrier, expected)
    for entry in (down[0], down_left, to_relay, side_low):
        start(entry)
    spectra((3, 1))
    spectra((2, 4, 7))
    start(side_high)
    start(side_right)

    small[2].wait()
    ra_step, dec_step = pairs_v[0, 1], pairs_v[0, 2]
    code = pairs_v[0, 0] * 5 + jnp.where(ra_step == 0, dec_step, dec_step + 3)
    slots = code.shape[1]
    hit = code == lax.broadcasted_iota(jnp.int32, (slots, slots), 0)
    slot_id = lax.broadcasted_iota(jnp.int32, (slots, slots), 1)
    inverse = jnp.max(jnp.where(hit, slot_id, 0), axis=1, keepdims=True)
    inv_v[...] = jnp.broadcast_to(inverse, inv_v.shape)
    to_smem.start()
    live_count = count[0, 0]

    blank = jnp.zeros((FPC, NPIX), BF16)
    for gone, cells in (
        (jnp.logical_not(above), [at(2, c) for c in range(5)]),
        (jnp.logical_not(above) | even, [at(2, -1)]),
        (even, [at(1, -1)]),
        (jnp.logical_not(right), [at(0, 4), at(1, 4)]),
        (jnp.logical_not(right) & above, [at(2, 4)]),
    ):
        @pl.when(gone)
        def _():
            for cell in cells:
                spec[cell] = blank
    acc[...] = jnp.zeros_like(acc)
    cacc[...] = jnp.zeros_like(cacc)

    spectra((5, 6))
    to_smem.wait()
    sep_load.wait()

    def code_of(row, col, offset):
        return (row * 4 + col) * 5 + offset

    def bins_of(code):
        slot = inv_s[code, 0]
        return (sep[slot] + jnp.where(slot < live_count, 0, 16)).astype(F32).astype(BF16)

    @pl.when(lend_bins[1])
    def _():
        ship[0] = bins_of(code_of(0, 0, 2))
        ship[1] = bins_of(code_of(1, 0, 2))
        lend_bins[0].start()

    def spread(which, k, counted, onehot):
        for t in range(NSEP):
            ones = jnp.where(which == jnp.asarray(t, BF16), jnp.asarray(1, BF16), jnp.asarray(0, BF16))
            onehot[pl.ds(t * FPC, FPC), pl.ds(k * FPC, FPC)] = ones
            if counted:
                cacc[t] += jnp.sum(ones.astype(F32).reshape(16, 8, FPC), axis=0)

    def multiply(a, b, n, acc):
        for m in range(NPIX // TILE):
            cols = pl.ds(m * TILE, TILE)
            partner = spec[pl.ds(b, n), :, cols].reshape(n * FPC, TILE)
            own = spec[a, :, cols].astype(F32).reshape(1, 16, 8, TILE)
            mixed = jnp.dot(onehot[:, :n * FPC], partner, preferred_element_type=F32)
            acc[:, :, cols] += jnp.sum(mixed.reshape(NSEP, 16, 8, TILE) * own, axis=1)

    def pair_up(a, b, first_code, n):
        for k in range(n):
            spread(bins_of(first_code + k), k, True, onehot)
        multiply(a, b, n, acc)

    column = lax.broadcasted_iota(jnp.int32, (NPIX, NKB), 0) % MODES
    in_bin = column // (MODES // NKB) == lax.broadcasted_iota(jnp.int32, (NPIX, NKB), 1)
    table = jnp.where(in_bin, 1.0, 0.0).astype(BF16)

    def fold(acc):
        rest = acc[...].reshape(NSEP * 8, NPIX)
        folded = jnp.zeros((NSEP * 8, NKB), F32)
        for _ in range(3):
            part = rest.astype(BF16)
            folded += jnp.dot(part, table, preferred_element_type=F32)
            rest = rest - part.astype(F32)
        return jnp.sum(folded.reshape(NSEP, 8, NKB), axis=1)

    @pl.loop(0, 6)
    def _(k):
        row, col = k // 3, k % 3
        pair_up(at(row, col), at(row, col), code_of(row, col, 0), 2)

    follow(down[0], down[3])
    arrived(at(0, -1), relay[1])
    start(relay)
    arrived(at(2, 0), above)
    for entry in (pass_up, pass_left):
        start(entry)

    @pl.loop(1, 3)
    def _(col):
        pair_up(at(0, col), at(1, col - 1), code_of(0, col, 2), 3)

    @pl.loop(0, 2)
    def _(k):
        col = 3 * k
        pair_up(at(0, col), at(1, col - k), code_of(0, col, 3 - k), 2)

    follow(down[3], down[1])
    arrived(at(2, 3), above)
    start(pass_right)
    arrived(at(1, 4), right)
    arrived(at(0, 4), right)

    @pl.when(give_back[1])
    def _():
        lend_bins[0].wait_recv()
        acc2[...] = jnp.zeros_like(acc2)

        @pl.loop(0, 2)
        def _(k):
            spread(shipped[k], 0, False, onehot)
            multiply(at(k, 4), at(k + 1, 3), 1, acc2)

        lent[...] = fold(acc2)
        give_back[0].start()

    @pl.loop(0, 2)
    def _(row):
        pair_up(at(row, 3), at(row, 3), code_of(row, 3, 0), 2)

    arrived(at(1, -1), odd)

    @pl.loop(0, 2)
    def _(k):
        col = 3 * k
        pair_up(at(0, col), at(1, col - 1 + 2 * k), code_of(0, col, 2 + 2 * k), 1)

    arrived(at(2, -1), above & odd)
    arrived(at(2, 4), above & right)

    @pl.loop(0, 2)
    def _(k):
        pair_up(at(1, 3 * k), at(2, 4 * k - 1), code_of(1, 3 * k, 2 + k), 2)

    follow(down[1], last[0])
    start(last[1])
    arrived(at(2, 1), above)

    @pl.loop(0, 2)
    def _(k):
        pair_up(at(1, 2 * k), at(2, 2 * k + 1), code_of(1, 2 * k, 4), 1)

    pair_up(at(1, 1), at(2, 0), code_of(1, 1, 2), 2)

    for k, (col, offset) in enumerate(((2, 2), (2, 3), (1, 4), (3, 2))):
        spread(bins_of(code_of(1, col, offset)), k, True, onehot2)
    for h in range(2):
        @pl.when(above)
        def _():
            last[h][0].wait_recv()

        @pl.loop(0, MODES // TILE)
        def _(m):
            cols = pl.ds(pl.multiple_of(h * MODES + m * TILE, TILE), TILE)
            total = acc[:, :, cols]
            for col, b, n, lane in ((2, 1, 2, 0), (1, 2, 1, 2), (3, 2, 1, 3)):
                partner = spec[pl.ds(at(2, b), n), :, cols].reshape(n * FPC, TILE)
                own = spec[at(1, col), :, cols].astype(F32).reshape(1, 16, 8, TILE)
                ones = onehot2[:, lane * FPC:(lane + n) * FPC]
                mixed = jnp.dot(ones, partner, preferred_element_type=F32)
                total += jnp.sum(mixed.reshape(NSEP, 16, 8, TILE) * own, axis=1)
            acc[:, :, cols] = total

    pay[0] = fold(acc)

    @pl.when(lend_bins[1])
    def _():
        give_back[0].wait_recv()
        pay[0] += lent_in[...]

    pay[1] = jnp.sum(cacc[...], axis=1)

    def everyone(source, box, mine, size, sent, got, peer):
        box[mine] = source[...]

        def copy(k):
            return pltpu.make_async_remote_copy(
                src_ref=source, dst_ref=box.at[mine], send_sem=sent.at[k], recv_sem=got.at[mine],
                device_id=peer(lax.rem(mine + k, size)), device_id_type=MESH)

        for k in sorted(range(1, size), key=lambda k: abs(2 * k - size)):
            copy(k).start()
        for k in range(1, size):
            other = lax.rem(mine + k, size)
            pltpu.make_async_remote_copy(
                src_ref=source, dst_ref=box.at[other], send_sem=sent.at[k], recv_sem=got.at[other],
                device_id=peer(other), device_id_type=MESH).wait_recv()
        total = box[0]
        for k in range(1, size):
            total = total + box[k]
        return total, [copy(k) for k in range(1, size)]

    total, first = everyone(pay, box1, q, n_dec, sent1, got1, lambda k: (p, k))
    pay2[...] = total
    total, second = everyone(pay2, box2, p, n_ra, sent2, got2, lambda k: (k, q))
    counts = jnp.sum(total[1], axis=1, keepdims=True)
    out[0] = pay[0]
    out[1] = total[0] / jnp.maximum(counts, 1.0)

    for copy in first + second:
        copy.wait_send()
    for copy, ok in [
        last[0], last[1], to_relay, relay, down_left, side_low, side_high, side_right, pass_left, pass_right, pass_up, lend_bins, give_back
    ]:
        @pl.when(ok)
        def _():
            copy.wait_send()


def per_device(n_ra, n_dec, forests, resolution, pixel_range, pairs, count, sep):
    vmem = pl.BlockSpec(memory_space=pltpu.VMEM)
    smem = pl.BlockSpec(memory_space=pltpu.SMEM)
    anywhere = pl.BlockSpec(memory_space=pl.ANY)
    dma = pltpu.SemaphoreType.DMA
    slots = pairs.shape[2]
    pairs = jnp.transpose(pairs, (0, 3, 1, 2))
    both = pl.pallas_call(
        functools.partial(kernel, n_ra, n_dec),
        out_shape=jax.ShapeDtypeStruct((2, NSEP, NKB), F32),
        in_specs=[anywhere, anywhere, anywhere, anywhere, smem, anywhere, anywhere],
        out_specs=vmem,
        scratch_shapes=[
            pltpu.VMEM((8, FPC, NPIX), BF16),
            pltpu.VMEM((NPIX, NPIX), BF16),
            pltpu.VMEM(sep.shape[2:], jnp.int32),
            pltpu.VMEM((3 * STRIDE, FPC, NPIX), BF16),
            pltpu.VMEM((3 * FPC, NPIX), BF16),
            pltpu.VMEM((NSEP * FPC, 3 * FPC), BF16),
            pltpu.VMEM((NSEP * FPC, 4 * FPC), BF16),
            pltpu.VMEM((NSEP, 8, NPIX), F32),
            pltpu.VMEM((NSEP, 8, NPIX), F32),
            pltpu.VMEM((NSEP, 8, FPC), F32),
            pltpu.VMEM((slots, 128), jnp.int32),
            pltpu.SMEM((slots, 128), jnp.int32),
            pltpu.VMEM((2, FPC, FPC), BF16),
            pltpu.VMEM((2, FPC, FPC), BF16),
            pltpu.VMEM((NSEP, NKB), F32),
            pltpu.VMEM((NSEP, NKB), F32),
            pltpu.VMEM((2, NSEP, NKB), F32),
            pltpu.VMEM((2, NSEP, NKB), F32),
            pltpu.VMEM((n_dec, 2, NSEP, NKB), F32),
            pltpu.VMEM((n_ra, 2, NSEP, NKB), F32),
            pltpu.VMEM(resolution.shape, F32),
            pltpu.VMEM(pixel_range.shape, jnp.int32),
            pltpu.VMEM(pairs.shape, jnp.int32),
            dma((14,)),
            dma((3 * STRIDE + 4,)),
            dma((17,)),
            dma((n_dec,)),
            dma((n_dec,)),
            dma((n_ra,)),
            dma((n_ra,)),
        ],
        compiler_params=pltpu.CompilerParams(
            collective_id=0, has_side_effects=True, vmem_limit_bytes=56 * 1024 * 1024
        ),
        cost_estimate=pl.CostEstimate(flops=13_000_000_000, bytes_accessed=7_000_000, transcendentals=500_000),
    )(forests, resolution, pixel_range, pairs, count, sep, jnp.asarray(dft_table()))
    return (both[0] * (1.0 / (FPC * NPIX))).reshape(1, 1, NSEP, NKB), both[1]


def solution(mesh):
    n_ra, n_dec = mesh.shape["ra"], mesh.shape["dec"]
    return jax.shard_map(
        functools.partial(per_device, n_ra, n_dec),
        mesh=mesh,
        in_specs=(
            P("ra", "dec", None, None),
            P("ra", "dec", None),
            P("ra", "dec", None, None),
            P("ra", "dec", None, None),
            P("ra", "dec"),
            P("ra", "dec", None, None, None),
        ),
        out_specs=(P("ra", "dec", None, None), P()),
        check_vma=False,
    )
```
